32 devices in a mesh: member: 2 (over x), lat: 16 (over z, y, core).
Axes of the slice: x: 2, y: 2, z: 4, core: 2. Of those that a mesh axis runs over, the one named last changes fastest.
Arguments:
- atmosphere: float32 [2, 4, 8, 96, 1536], P(None, 'member', None, 'lat'), may hold values from -4 to 4
- ocean_state: float32 [2, 96, 1536], P(None, 'lat', 'member'), may hold values from -4 to 4
- viscosity: float32 [96, 1536], P('lat', 'member'), may hold values from 0.02 to 0.2
- sea_mask: int32 [96, 1536], P('lat'), may hold values 0 or 1
- parameter_index: int32 [4], P('member'), may hold values from 0 to 31
- parameter_table: float32 [32, 3], replicated, may hold values from 0.1 to 0.3
- level_mix: float32 [8, 8], replicated, may hold values from -0.5 to 0.5
Outputs:
- atmos_out: float32 [2, 4, 8, 96, 1536], P(None, 'member', None, 'lat')
- ocean_out: float32 [2, 96, 1536], P(None, 'lat', 'member')
The draws below stay inside these ranges and needn't reach their ends.
All inputs are finite; a program needn't handle non-finite values. No bound on the sum of `sea_mask` on one device may be relied on, other than what follows from the above.
Results may differ from the reference program's by a relative error of at most 0.00011.
Values sent between devices are 32-bit elements; how exact they have to be, the bound alone decides.
No kernel may reach another device: no remote copies, remote signals or barrier semaphores. Data moves between devices by JAX's collectives and lax.ppermute only.
A program may use at most 64 MiB of HBM per device.

```python
import math
import jax
import jax.numpy as jnp
from jax import lax

LEV = 8
LON = 1536
SETS = 32
PCOUNT = 3
ASTEPS = 3
OSTEPS = 2
COUPLE = 2
MEMBERS = 4
NLAT = 96


def touch_ends(drawn, stream_key, low, high):
    spot = [jax.random.randint(jax.random.fold_in(stream_key, axis), (), 0, length) for axis, length in enumerate(drawn.shape)]
    longest = drawn.shape.index(max(drawn.shape))
    beside = spot[:longest] + [(spot[longest] + 1) % drawn.shape[longest]] + spot[longest + 1:]
    return drawn.at[tuple(spot)].set(low).at[tuple(beside)].set(high)


def block_levels(key, extent, split, least, largest):
    loudness = 1.0
    for position, parts in split:
        heights = jax.random.uniform(jax.random.fold_in(jax.random.fold_in(key, 6), position), (parts,), jnp.float32, least / len(split), largest / len(split))
        loudness = loudness * jnp.repeat(jnp.exp(heights), extent[position] // parts).reshape((-1,) + (1,) * (len(extent) - 1 - position))
    return loudness


def bell_draw(own_key, extent, deviation, bound, cuts=(), kind=jnp.bfloat16):
    drawn = jax.random.normal(own_key, extent, jnp.float32) * deviation
    if len(cuts) > 0:
        drawn = block_levels(own_key, extent, cuts, -0.22, 0.18) * drawn
    return jnp.clip(drawn, min=-bound, max=bound).astype(kind)


def setup_inputs(seed: int = 0) -> dict:
    key_of = jax.random.split(jax.random.key(seed), 8)
    return {
        "atmosphere": bell_draw(key_of[0], (2, MEMBERS, LEV, NLAT, LON), 1.0, 4.0, ((1, 2), (3, 16)), jnp.float32),
        "ocean_state": bell_draw(key_of[1], (2, NLAT, LON), 1.0, 4.0, ((1, 16), (2, 2)), jnp.float32),
        "viscosity": jnp.clip(jnp.exp(math.log(0.2) - 2.3025851 * jax.random.uniform(key_of[2], (NLAT, LON), jnp.float32) ** block_levels(key_of[2], (NLAT, LON), ((0, 16), (1, 2)), -0.2, 0.2)), 0.02, 0.2),
        "sea_mask": touch_ends((jax.random.randint(key_of[3], (NLAT, LON), 0, 3) < 2).astype(jnp.int32), jax.random.fold_in(key_of[3], 1), 0, 1),
        "parameter_index": touch_ends(jax.random.randint(key_of[4], (MEMBERS,), 0, SETS), jax.random.fold_in(key_of[4], 1), 0, SETS - 1).astype(jnp.int32),
        "parameter_table": jnp.clip(jnp.exp(jax.random.uniform(key_of[5], (SETS, PCOUNT), jnp.float32, math.log(0.1), math.log(0.3))), 0.1, 0.3),
        "level_mix": bell_draw(key_of[6], (LEV, LEV), 0.1, 0.5, (), jnp.float32),
    }


ADVECTION = 0.1
OCEAN_GAIN = 0.5
OCEAN_DIFFUSION = 0.15


def lookup(parameter_index, parameter_table):
    onehot = (parameter_index[:, None] == jnp.arange(parameter_table.shape[0], dtype=jnp.int32)[None, :]).astype(jnp.float32)
    picked = jnp.dot(onehot, parameter_table, precision=lax.Precision.HIGHEST, preferred_element_type=jnp.float32)
    return 0.6 * picked[:, 0], 2.0 * jnp.transpose(picked[:, 1:3])


def atmos_step(padded_rows, surface, diffusivity, exchange, level_mix):
    centre = padded_rows[:, :, :, 1:-1, :]
    northern = padded_rows[:, :, :, 2:, :]
    southern = padded_rows[:, :, :, :-2, :]
    eastern = jnp.roll(centre, -1, axis=4)
    western = jnp.roll(centre, 1, axis=4)
    laplace = eastern + western + northern + southern - 4.0 * centre
    zonal_wind = centre[1]
    advected = centre - ADVECTION * zonal_wind[None] * (eastern - western) * 0.5 + diffusivity[None, :, None, None, None] * laplace
    mixed_state = advected + jnp.einsum("kl,fmlrn->fmkrn", level_mix, advected, precision=lax.Precision.HIGHEST)
    bottom = mixed_state[:, :, 0] + exchange[:, :, None, None] * (surface[:, None] - mixed_state[:, :, 0])
    return mixed_state.at[:, :, 0].set(bottom)


def reference(atmosphere, ocean_state, viscosity, sea_mask, parameter_index, parameter_table, level_mix):
    diffusivity, exchange = lookup(parameter_index, parameter_table)
    ocean_mask = sea_mask.astype(jnp.float32)
    ocean_rate = jnp.stack([jnp.full_like(viscosity, OCEAN_DIFFUSION), viscosity])
    atmos_state = atmosphere
    ocean = ocean_state
    for coupling in range(COUPLE):
        surface = ocean
        for substep in range(ASTEPS):
            padded_rows = jnp.pad(atmos_state, ((0, 0), (0, 0), (0, 0), (1, 1), (0, 0)))
            atmos_state = atmos_step(padded_rows, surface, diffusivity, exchange, level_mix)
        flux_terms = jnp.sum(exchange[:, :, None, None] * (atmos_state[:, :, 0] - surface[:, None]), axis=1)
        forcing = flux_terms / MEMBERS
        for substep in range(OSTEPS):
            padded_ocean = jnp.pad(ocean, ((0, 0), (1, 1), (0, 0)))
            laplace = padded_ocean[:, 2:] + padded_ocean[:, :-2] + jnp.roll(ocean, -1, axis=2) + jnp.roll(ocean, 1, axis=2) - 4.0 * ocean
            ocean = ocean + ocean_mask[None] * (OCEAN_GAIN * forcing + ocean_rate * laplace)
    return atmos_state, ocean
```

```python
import functools

import jax
import jax.numpy as jnp
from jax import lax
from jax.experimental import pallas as pl
from jax.experimental.pallas import tpu as pltpu
from jax.sharding import PartitionSpec as P

ASTEPS = 3
OSTEPS = 2
COUPLE = 2

ADVECTION = 0.1
OCEAN_GAIN = 0.5
OCEAN_DIFFUSION = 0.15

ANY = pl.BlockSpec(memory_space=pl.ANY)
VMEM = pl.BlockSpec(memory_space=pltpu.VMEM)
SMEM = pl.BlockSpec(memory_space=pltpu.SMEM)
LANES = 128


def place(up, row, base, count):
    return jnp.where(up == 1, row - base, count - 1 - (row - base))


def chunk(up, row, length, base, count):
    return jnp.where(up == 1, row - base, count - length - (row - base))


class Sems:
    def __init__(self, sems):
        self.sems, self.used = sems, 0

    def copies(self):
        return Group(self)


class Group:
    def __init__(self, owner):
        self.owner, self.started = owner, []

    def start(self, source, target):
        copy = pltpu.make_async_copy(source, target, self.owner.sems.at[self.owner.used])
        self.owner.used += 1
        copy.start()
        self.started.append(copy)

    def wait(self):
        for copy in self.started:
            copy.wait()


def atmos_rows(up, reals, coef, source, target, surface, first, count, edge, valid):
    src, src_base, src_rows = source
    dst, dst_base, dst_rows = target
    srf, srf_base, srf_rows = surface
    members, lon = src.shape[1], src.shape[4]
    level = lax.broadcasted_iota(jnp.int32, (8, LANES), 0)

    def one(i, carry):
        row = first + i
        here = place(up, row, src_base, src_rows)
        there = place(up, row, dst_base, dst_rows)
        sea = place(up, row, srf_base, srf_rows)
        for m in range(members):
            diffusivity = reals[m]
            keep = 1.0 - 4.0 * diffusivity
            wind = None
            for c in (1, 0):
                centre = src[c, m, here]
                if wind is None:
                    wind = (0.5 * ADVECTION) * centre
                eastern = pltpu.roll(centre, lon - 1, 1)
                western = pltpu.roll(centre, 1, 1)
                beside = src[c, m, here - 1] + src[c, m, here + 1]
                advected = (
                    keep * centre
                    + diffusivity * (beside + (eastern + western))
                    - wind * (eastern - western)
                )
                relax = jnp.where(level == 0, reals[members + c * members + m], 0.0)
                for t in range(lon // LANES):
                    part = advected[:, t * LANES : (t + 1) * LANES]
                    total = coef[c, m, 0] * part
                    for d in range(1, 8):
                        total += coef[c, m, d] * pltpu.roll(part, 8 - d, 0)
                    total += relax * srf[sea, c : c + 1, t * LANES : (t + 1) * LANES]
                    if edge is not None:
                        total = total * jnp.where(row >= edge, valid, 1.0)
                    dst[c, m, there, :, t * LANES : (t + 1) * LANES] = total
        return carry

    lax.fori_loop(0, count, one, 0)


def flux_rows(up, reals, state, surface, out, first, count, ensemble):
    st, st_base, st_rows = state
    srf, srf_base, srf_rows = surface
    ref, base, rows = out
    members = st.shape[1]

    def one(i, carry):
        row = first + i
        at = place(up, row, st_base, st_rows)
        sea = place(up, row, srf_base, srf_rows)
        to = place(up, row, base, rows)
        for c in range(2):
            s = srf[sea, c : c + 1, :]
            flux = jnp.zeros_like(s)
            for m in range(members):
                flux += reals[members + c * members + m] * (st[c, m, at, 0:1, :] - s)
            ref[to, c : c + 1, :] = flux * (1.0 / ensemble)
        return carry

    lax.fori_loop(0, count, one, 0)


def ocean_rows(up, sea, ocean, forcing, target, first, count):
    src, src_base, src_rows = ocean
    fixed, fixed_base, fixed_rows = sea
    frc, frc_base, frc_rows = forcing
    dst, dst_base, dst_rows = target
    lon = src.shape[2]

    def one(i, carry):
        row = first + i
        here = place(up, row, src_base, src_rows)
        cell = place(up, row, fixed_base, fixed_rows)
        force = place(up, row, frc_base, frc_rows)
        to = place(up, row, dst_base, dst_rows)
        mask = fixed[cell, 3:4, :]
        for c in range(2):
            centre = src[here, c : c + 1, :]
            laplace = (
                (pltpu.roll(centre, lon - 1, 1) + pltpu.roll(centre, 1, 1))
                + (src[here - 1, c : c + 1, :] + src[here + 1, c : c + 1, :])
                - 4.0 * centre
            )
            rate = OCEAN_DIFFUSION if c == 0 else fixed[cell, 2:3, :]
            dst[to, c : c + 1, :] = centre + mask * (OCEAN_GAIN * frc[force, c : c + 1, :] + rate * laplace)
        return carry

    lax.fori_loop(0, count, one, 0)


def load_three(up, group, target, band, low, own, high):
    group.start(low, target.at[pl.ds(jnp.where(up == 1, 0, 2 * band), band)])
    group.start(own, target.at[pl.ds(band, band)])
    group.start(high, target.at[pl.ds(jnp.where(up == 1, 2 * band, 0), band)])


def inner_kernel(cfg, coupled, *refs):
    band, H, ensemble = cfg
    refs = list(refs)
    sems = refs.pop()
    ints, reals, coef, a_low, a_in, a_out, sea_low, sea_own, sea_high = refs[:9]
    del refs[:9]
    if coupled:
        f_low, f_own, f_high = refs[:3]
        del refs[:3]
        done, carry1, carry2, flux, surface_out = refs[:5]
        del refs[:5]
    else:
        done, carry1, carry2, flux = refs[:4]
        del refs[:4]
    win, lev1, lev2, sea = refs[:4]
    del refs[:4]
    up = ints[0]
    pool = Sems(sems)
    loads = pool.copies()
    size = 3 * H
    loads.start(a_low, win.at[:, :, pl.ds(chunk(up, -H, H, -H, size), H)])
    loads.start(a_in, win.at[:, :, pl.ds(chunk(up, 0, H, -H, size), H)])
    loads.start(a_out, win.at[:, :, pl.ds(chunk(up, H, H, -H, size), H)])
    load_three(up, loads, sea, band, sea_low, sea_own, sea_high)
    whole = 3 * band
    if coupled:
        force, middle, surf = refs
        load_three(up, loads, force, band, f_low, f_own, f_high)
    loads.wait()
    fixed = (sea, -band, whole)
    if coupled:
        forcing, half = (force, -band, whole), (middle, -band, whole)
        ocean_rows(up, fixed, fixed, forcing, half, -H, 2 * H + 3)
        surface = (surf, -band, whole)
        ocean_rows(up, fixed, half, forcing, surface, -H + 1, 2 * H + 1)
    else:
        surface = fixed
    step0, step1, step2 = (win, -H, size), (lev1, 1 - H, 7), (lev2, 2 - H, 5)
    step3 = (done, 0, H)
    atmos_rows(up, reals, coef, step0, step1, surface, 1 - H, 7, None, None)
    atmos_rows(up, reals, coef, step1, step2, surface, 2 - H, 5, None, None)
    atmos_rows(up, reals, coef, step2, step3, surface, 0, 3, None, None)
    stores = pool.copies()
    stores.start(lev1.at[:, :, pl.ds(chunk(up, 3, 2, 1 - H, 7), 2)], carry1)
    stores.start(lev2.at[:, :, pl.ds(chunk(up, 2, 2, 2 - H, 5), 2)], carry2)
    if coupled:
        stores.start(surf, surface_out)
    flux_rows(up, reals, step3, surface, (flux, 0, H), 0, H, ensemble)
    stores.wait()


def tile(up, reals, coef, win, lev1, lev2, target, base, surface, edge, valid):
    atmos_rows(up, reals, coef, (win, base - 1, 5), (lev1, base - 2, 5), surface, base, 3, edge, valid)
    atmos_rows(up, reals, coef, (lev1, base - 2, 5), (lev2, base - 3, 5), surface, base - 1, 3, edge, valid)
    atmos_rows(up, reals, coef, (lev2, base - 3, 5), target, surface, base - 2, 3, edge, valid)


def outer_kernel(cfg, ints, reals, coef, a_out, a_high, carry1, carry2, flux_in, sea_low, sea_own, sea_high,
                 done, next1, next2, flux, win, lev1, lev2, sea, sems):
    band, H, ensemble = cfg
    up, valid = ints[0], reals[reals.shape[0] - 1]
    pool = Sems(sems)
    loads = pool.copies()
    loads.start(a_out.at[:, :, pl.ds(chunk(up, 4, 2, 3, 3), 2)], win.at[:, :, pl.ds(chunk(up, 4, 2, 4, 5), 2)])
    loads.start(a_high, win.at[:, :, pl.ds(chunk(up, 6, 3, 4, 5), 3)])
    loads.start(carry1, lev1.at[:, :, pl.ds(chunk(up, 3, 2, 3, 5), 2)])
    loads.start(carry2, lev2.at[:, :, pl.ds(chunk(up, 2, 2, 2, 5), 2)])
    load_three(up, loads, sea, band, sea_low, sea_own, sea_high)
    loads.start(flux_in, flux.at[pl.ds(chunk(up, 0, H, 0, band), H)])
    loads.wait()
    surface = (sea, -band, 3 * band)
    tile(up, reals, coef, win, lev1, lev2, (done, 3, 3), 5, surface, band, valid)
    stores = pool.copies()
    stores.start(lev1.at[:, :, pl.ds(chunk(up, 6, 2, 3, 5), 2)], next1)
    stores.start(lev2.at[:, :, pl.ds(chunk(up, 5, 2, 2, 5), 2)], next2)
    flux_rows(up, reals, (done, 3, 3), surface, (flux, 0, band), 3, 3, ensemble)
    stores.wait()


def last_kernel(cfg, ints, reals, coef, a_high, a_far, carry1, carry2, sea_low, sea_own, sea_high,
                f_low, f_own, f_high, b_out, b_in, b_carry1, b_carry2, flux_in,
                result, flux, surface_out, win, lev1, lev2, win_b, lev1_b, lev2_b, done, sea, force, middle, surf, sems):
    band, H, ensemble = cfg
    up, valid = ints[0], reals[reals.shape[0] - 1]
    pool = Sems(sems)
    loads = pool.copies()
    whole = 3 * band
    loads.start(a_high.at[:, :, pl.ds(chunk(up, 7, 2, 6, 3), 2)], win.at[:, :, pl.ds(chunk(up, 7, 2, 7, 5), 2)])
    loads.start(a_far, win.at[:, :, pl.ds(chunk(up, 9, 3, 7, 5), 3)])
    loads.start(carry1, lev1.at[:, :, pl.ds(chunk(up, 6, 2, 6, 5), 2)])
    loads.start(carry2, lev2.at[:, :, pl.ds(chunk(up, 5, 2, 5, 5), 2)])
    load_three(up, loads, sea, band, sea_low, sea_own, sea_high)
    load_three(up, loads, force, band, f_low, f_own, f_high)
    loads.start(b_out.at[:, :, pl.ds(chunk(up, 4, 2, 3, 3), 2)], win_b.at[:, :, pl.ds(chunk(up, 4, 2, 4, 5), 2)])
    loads.start(b_carry1, lev1_b.at[:, :, pl.ds(chunk(up, 3, 2, 3, 5), 2)])
    loads.start(b_carry2, lev2_b.at[:, :, pl.ds(chunk(up, 2, 2, 2, 5), 2)])
    loads.start(flux_in, flux.at[pl.ds(chunk(up, 0, H, 0, band), H)])
    loads.wait()
    stores = pool.copies()
    stores.start(b_in, result.at[:, :, pl.ds(chunk(up, 0, H, 0, band), H)])
    fixed, forcing, half = (sea, -band, whole), (force, -band, whole), (middle, -band, whole)
    surface = (surf, -band, whole)
    ocean_rows(up, fixed, fixed, forcing, half, -3, 12)
    ocean_rows(up, fixed, half, forcing, surface, -2, 10)
    tile(up, reals, coef, win, lev1, lev2, (win_b, 4, 5), 8, fixed, band, valid)
    tile(up, reals, coef, win_b, lev1_b, lev2_b, (done, 3, 3), 5, surface, band, valid)
    stores.start(done, result.at[:, :, pl.ds(chunk(up, 3, H, 0, band), H)])
    stores.start(surf, surface_out)
    flux_rows(up, reals, (done, 3, 3), surface, (flux, 0, band), 3, 3, ensemble)
    stores.wait()


def ocean_kernel(cfg, ints, surface_in, sea_low, sea_own, sea_high, f_low, f_own, f_high, out,
                 sea, surf, force, middle, final, sems):
    band, H, tile_width = cfg
    up = ints[0]
    pool = Sems(sems)
    loads = pool.copies()
    whole = 3 * band
    load_three(up, loads, sea, band, sea_low, sea_own, sea_high)
    loads.start(surface_in, surf)
    loads.start(f_low, force.at[pl.ds(chunk(up, -1, 1, -1, band + 2), 1)])
    loads.start(f_own, force.at[pl.ds(1, band)])
    loads.start(f_high, force.at[pl.ds(chunk(up, band, 1, -1, band + 2), 1)])
    loads.wait()
    fixed, ocean = (sea, -band, whole), (surf, -band, whole)
    forcing, half = (force, -1, band + 2), (middle, -1, band + 2)
    ocean_rows(up, fixed, ocean, forcing, half, -1, band + 2)
    ocean_rows(up, fixed, half, forcing, (final, 0, band), 0, band)
    if tile_width is None:
        out[...] = final[...]
    else:
        out[...] = final[:, :, pl.ds(pl.multiple_of(ints[1] * tile_width, LANES), tile_width)]


def call(kernel, name, outs, scratch, args, copies, flops=0):
    kinds = {"any": ANY, "vmem": VMEM, "smem": SMEM}
    return pl.pallas_call(
        kernel,
        name=name,
        out_shape=[jax.ShapeDtypeStruct(shape, jnp.float32) for _, shape in outs],
        in_specs=[kinds[kind] for kind, _ in args],
        out_specs=[kinds[kind] for kind, _ in outs],
        scratch_shapes=[pltpu.VMEM(shape, jnp.float32) for shape in scratch] + [pltpu.SemaphoreType.DMA((copies,))],
        compiler_params=pltpu.CompilerParams(vmem_limit_bytes=24 * 1024 * 1024),
        cost_estimate=pl.CostEstimate(flops=flops, bytes_accessed=4 * 1024 * 1024, transcendentals=0),
    )(*[value for _, value in args])


def lookup(parameter_index, parameter_table):
    onehot = (
        parameter_index[:, None] == jnp.arange(parameter_table.shape[0], dtype=jnp.int32)[None, :]
    ).astype(jnp.float32)
    picked = jnp.dot(
        onehot, parameter_table, precision=lax.Precision.HIGHEST, preferred_element_type=jnp.float32
    )
    return (0.6 * picked[:, 0], 2.0 * jnp.transpose(picked[:, 1:3]))


def mixing(level_mix, exchange):
    levels = level_mix.shape[0]
    ids = jnp.arange(levels)
    pick = (ids[None, None, :] == (ids[None, :, None] + ids[:, None, None]) % levels).astype(jnp.float32)
    whole = level_mix + jnp.eye(levels, dtype=jnp.float32)
    turned = jnp.sum(pick * whole[None], axis=2)
    scale = jnp.where(ids == 0, 1.0 - exchange[:, :, None], 1.0)
    coef = turned[None, None] * scale[:, :, None, :]
    return jnp.broadcast_to(coef[..., None], coef.shape + (LANES,))


def body(atmosphere, ocean_state, viscosity, sea_mask, parameter_index, parameter_table, level_mix):
    H = ASTEPS
    fields, members, levels, band, lon = atmosphere.shape
    width = ocean_state.shape[2]
    sides, bands = lax.axis_size("member"), lax.axis_size("lat")
    ensemble = members * sides
    position = lax.axis_index("lat")
    side = lax.axis_index("member")
    up = position % 2
    near = [(i, i + 1) for i in range(0, bands, 2)]
    near += [(b, a) for a, b in near]
    far = [(i, i + 1) for i in range(1, bands - 1, 2)]
    far += [(b, a) for a, b in far]
    other = [(0, 1), (1, 0)]

    def to_near(x):
        return lax.ppermute(x, "lat", near)

    def to_far(x):
        return lax.ppermute(x, "lat", far)

    def total(x):
        if sides == 2:
            return x + lax.ppermute(x, "member", other)
        return lax.psum(x, "member")

    def full_rows(x):
        if sides == 2:
            y = lax.ppermute(x, "member", other)
            low, high = jnp.where(side == 0, x, y), jnp.where(side == 0, y, x)
            return jnp.concatenate([low, high], axis=2)
        return lax.all_gather(x, "member", axis=2, tiled=True)

    state = jnp.transpose(atmosphere, (0, 1, 3, 2, 4))
    a_out = lax.dynamic_slice_in_dim(state, up * H, H, 2)
    a_high = to_far(a_out)
    a_in = lax.dynamic_slice_in_dim(state, (1 - up) * H, H, 2)
    a_low = to_near(a_in)

    tile_fields = jnp.concatenate([jnp.transpose(ocean_state, (1, 0, 2)), viscosity[:, None]], axis=1)
    sea_own = jnp.concatenate([full_rows(tile_fields), sea_mask.astype(jnp.float32)[:, None]], axis=1)
    sea_low, sea_high = to_near(sea_own), to_far(sea_own)

    diffusivity, exchange = lookup(parameter_index, parameter_table)
    coef = mixing(level_mix, exchange)
    valid = jnp.where(up == 1, position < bands - 1, position > 0).astype(jnp.float32)
    reals = jnp.concatenate([diffusivity, exchange.reshape(-1), valid[None]])
    ints = jnp.stack([up, side]).astype(jnp.int32)
    common = [("smem", ints), ("smem", reals), ("vmem", coef)]
    seas = [("any", sea_low), ("any", sea_own), ("any", sea_high)]

    def rows(n):
        return (fields, members, n, levels, lon)

    cfg = (band, H, ensemble)
    unit = members * fields * levels * lon * 30

    def inner(coupled, low, inside, outside, sea3, force3, name):
        outs = [("vmem", rows(H)), ("any", rows(2)), ("any", rows(2)), ("vmem", (H, fields, lon))]
        scratch = [rows(3 * H), rows(7), rows(5), (3 * band, 4, lon)]
        if coupled:
            scratch += [(3 * band, 2, lon)] * 3
            outs += [("any", (3 * band, 2, lon))]
        args = common + [("any", low), ("any", inside), ("any", outside)] + sea3 + force3
        return call(functools.partial(inner_kernel, cfg, coupled), name, outs, scratch, args, 16, 15 * unit)

    b_in, carry1, carry2, flux = inner(False, a_low, a_in, a_out, seas[:2] + [("any", sea_own)], [], "inner_first")
    a_far = to_far(a_in)
    b_low = to_near(b_in)
    b_out, carry1, carry2, flux = call(
        functools.partial(outer_kernel, cfg), "outer_first",
        [("vmem", rows(H)), ("any", rows(2)), ("any", rows(2)), ("vmem", (band, fields, lon))],
        [rows(5), rows(5), rows(5), (3 * band, 4, lon)],
        common + [("any", a_out), ("any", a_high), ("any", carry1), ("any", carry2), ("any", flux)] + seas, 16, 9 * unit)
    f_own = total(flux)
    f_low, f_high = to_near(f_own), to_far(f_own)
    c_in, b_carry1, b_carry2, flux, _ = inner(
        True, b_low, b_in, b_out, seas,
        [("any", f_low), ("any", f_own), ("any", f_own)], "inner_second")
    result, flux, surface = call(
        functools.partial(last_kernel, cfg), "outer_second",
        [("any", rows(band)), ("vmem", (band, fields, lon)), ("any", (3 * band, 2, lon))],
        [rows(5)] * 6 + [rows(H), (3 * band, 4, lon)] + [(3 * band, 2, lon)] * 3,
        common + [("any", a_high), ("any", a_far), ("any", carry1), ("any", carry2)] + seas
        + [("any", f_low), ("any", f_own), ("any", f_high), ("any", b_out), ("any", c_in), ("any", b_carry1), ("any", b_carry2), ("any", flux)],
        24, 18 * unit)
    g_own = total(flux)
    g_low = to_near(lax.dynamic_slice_in_dim(g_own, (1 - up) * (band - 1), 1, 0))
    g_high = to_far(lax.dynamic_slice_in_dim(g_own, up * (band - 1), 1, 0))
    inside_kernel = width % LANES == 0
    (ocean,) = call(
        functools.partial(ocean_kernel, (band, H, width if inside_kernel else None)), "ocean_last",
        [("vmem", (band, fields, width if inside_kernel else lon))],
        [(3 * band, 4, lon), (3 * band, 2, lon), (band + 2, 2, lon), (band + 2, 2, lon), (band, 2, lon)],
        [("smem", ints), ("any", surface)] + seas + [("any", g_low), ("any", g_own), ("any", g_high)], 8)
    if not inside_kernel:
        ocean = lax.dynamic_slice_in_dim(ocean, side * width, width, 2)
    return (jnp.transpose(result, (0, 1, 3, 2, 4)), jnp.transpose(ocean, (1, 0, 2)))


def solution(mesh):
    return jax.shard_map(
        body,
        mesh=mesh,
        in_specs=(
            P(None, "member", None, "lat", None),
            P(None, "lat", "member"),
            P("lat", "member"),
            P("lat", None),
            P("member"),
            P(),
            P(),
        ),
        out_specs=(P(None, "member", None, "lat", None), P(None, "lat", "member")),
        check_vma=False,
    )
```

```python
import functools

import jax
import jax.numpy as jnp
from jax import lax
from jax.experimental import pallas as pl
from jax.experimental.pallas import tpu as pltpu
from jax.sharding import PartitionSpec as P

ASTEPS = 3
OSTEPS = 2
COUPLE = 2

ADVECTION = 0.1
OCEAN_GAIN = 0.5
OCEAN_DIFFUSION = 0.15

ANY = pl.BlockSpec(memory_space=pl.ANY)
VMEM = pl.BlockSpec(memory_space=pltpu.VMEM)
SMEM = pl.BlockSpec(memory_space=pltpu.SMEM)
LANES = 128
QUARTERS = 4


def place(up, row, base, count):
    return jnp.where(up == 1, row - base, count - 1 - (row - base))


def chunk(up, row, length, base, count):
    return jnp.where(up == 1, row - base, count - length - (row - base))


class Sems:
    def __init__(self, sems):
        self.sems, self.used = sems, 0

    def copies(self):
        return Group(self)


class Group:
    def __init__(self, owner):
        self.owner, self.started = owner, []

    def start(self, source, target):
        copy = pltpu.make_async_copy(source, target, self.owner.sems.at[self.owner.used])
        self.owner.used += 1
        copy.start()
        self.started.append(copy)

    def wait(self):
        for copy in self.started:
            copy.wait()


def sea_piece(ref, row, c, t, lon):
    per = lon // QUARTERS // LANES
    line, part = c * QUARTERS + t // per, t % per
    return ref[row, line : line + 1, part * LANES : (part + 1) * LANES]


def atmos_rows(up, reals, coef, source, target, surface, first, count, edge, valid):
    src, src_base, src_rows = source
    dst, dst_base, dst_rows = target
    srf, srf_base, srf_rows = surface
    members, lon = src.shape[1], src.shape[4]
    level = lax.broadcasted_iota(jnp.int32, (8, LANES), 0)

    def one(i, carry):
        row = first + i
        here = place(up, row, src_base, src_rows)
        there = place(up, row, dst_base, dst_rows)
        sea = place(up, row, srf_base, srf_rows)
        for m in range(members):
            diffusivity = reals[m]
            keep = 1.0 - 4.0 * diffusivity
            wind = None
            for c in (1, 0):
                centre = src[c, m, here]
                if wind is None:
                    wind = (0.5 * ADVECTION) * centre
                eastern = pltpu.roll(centre, lon - 1, 1)
                western = pltpu.roll(centre, 1, 1)
                beside = src[c, m, here - 1] + src[c, m, here + 1]
                advected = (
                    keep * centre
                    + diffusivity * (beside + (eastern + western))
                    - wind * (eastern - western)
                )
                relax = jnp.where(level == 0, reals[members + c * members + m], 0.0)
                for t in range(lon // LANES):
                    part = advected[:, t * LANES : (t + 1) * LANES]
                    total = coef[c, m, 0] * part
                    for d in range(1, 8):
                        total += coef[c, m, d] * pltpu.roll(part, 8 - d, 0)
                    total += relax * sea_piece(srf, sea, c, t, lon)
                    if edge is not None:
                        total = total * jnp.where(row >= edge, valid, 1.0)
                    dst[c, m, there, :, t * LANES : (t + 1) * LANES] = total
        return carry

    lax.fori_loop(0, count, one, 0)


def flux_rows(up, reals, state, surface, out, first, count, ensemble):
    st, st_base, st_rows = state
    srf, srf_base, srf_rows = surface
    ref, base, rows = out
    members, lon = st.shape[1], st.shape[4]

    def one(i, carry):
        row = first + i
        at = place(up, row, st_base, st_rows)
        sea = place(up, row, srf_base, srf_rows)
        to = place(up, row, base, rows)
        per = lon // QUARTERS // LANES
        for c in range(2):
            for t in range(lon // LANES):
                s = sea_piece(srf, sea, c, t, lon)
                flux = jnp.zeros_like(s)
                for m in range(members):
                    flux += reals[members + c * members + m] * (st[c, m, at, 0:1, t * LANES : (t + 1) * LANES] - s)
                line, part = c * QUARTERS + t // per, t % per
                ref[to, line : line + 1, part * LANES : (part + 1) * LANES] = flux * (1.0 / ensemble)
        return carry

    lax.fori_loop(0, count, one, 0)


def ocean_rows(up, sea, ocean, forcing, target, first, count):
    src, src_base, src_rows = ocean
    fixed, fixed_base, fixed_rows = sea
    frc, frc_base, frc_rows = forcing
    dst, dst_base, dst_rows = target
    lines, lon = src.shape[1:]
    line = lax.broadcasted_iota(jnp.int32, (lines, lon), 0)
    lane = lax.broadcasted_iota(jnp.int32, (lines, lon), 1)
    quarter = line % QUARTERS

    for i in range(count):
        row = first + i
        here = place(up, row, src_base, src_rows)
        cell = place(up, row, fixed_base, fixed_rows)
        force = place(up, row, frc_base, frc_rows)
        to = place(up, row, dst_base, dst_rows)
        both = fixed[cell]
        turned = pltpu.roll(both, QUARTERS, 0)
        mask = jnp.where(line < QUARTERS, turned, both)
        rate = jnp.where(line < QUARTERS, OCEAN_DIFFUSION, turned)
        centre = src[here]
        eastern, western = pltpu.roll(centre, lon - 1, 1), pltpu.roll(centre, 1, 1)
        after = jnp.where(quarter == QUARTERS - 1, pltpu.roll(eastern, QUARTERS - 1, 0), pltpu.roll(eastern, lines - 1, 0))
        before = jnp.where(quarter == 0, pltpu.roll(western, lines - QUARTERS + 1, 0), pltpu.roll(western, 1, 0))
        eastern = jnp.where(lane == lon - 1, after, eastern)
        western = jnp.where(lane == 0, before, western)
        laplace = (eastern + western) + (src[here - 1] + src[here + 1]) - 4.0 * centre
        dst[to] = centre + mask * (OCEAN_GAIN * frc[force] + rate * laplace)


def load_three(up, group, target, band, low, own, high):
    group.start(low, target.at[pl.ds(jnp.where(up == 1, 0, 2 * band), band)])
    group.start(own, target.at[pl.ds(band, band)])
    group.start(high, target.at[pl.ds(jnp.where(up == 1, 2 * band, 0), band)])


def inner_kernel(cfg, coupled, *refs):
    band, H, ensemble = cfg
    refs = list(refs)
    sems = refs.pop()
    ints, reals, coef, a_low, a_in, a_out, sea_low, sea_own, sea_high = refs[:9]
    del refs[:9]
    if coupled:
        f_low, f_own, f_high = refs[:3]
        del refs[:3]
        done, carry1, carry2, flux, surface_out = refs[:5]
        del refs[:5]
    else:
        done, carry1, carry2, flux = refs[:4]
        del refs[:4]
    win, lev1, lev2, sea = refs[:4]
    del refs[:4]
    up = ints[0]
    pool = Sems(sems)
    loads = pool.copies()
    size = 3 * H
    loads.start(a_low, win.at[:, :, pl.ds(chunk(up, -H, H, -H, size), H)])
    loads.start(a_in, win.at[:, :, pl.ds(chunk(up, 0, H, -H, size), H)])
    loads.start(a_out, win.at[:, :, pl.ds(chunk(up, H, H, -H, size), H)])
    load_three(up, loads, sea, band, sea_low, sea_own, sea_high)
    whole = 3 * band
    if coupled:
        force, middle, surf = refs
        load_three(up, loads, force, band, f_low, f_own, f_high)
    loads.wait()
    start, fixed = (sea.at[:, 0], -band, whole), (sea.at[:, 1], -band, whole)
    if coupled:
        forcing, half = (force, -band, whole), (middle, -band, whole)
        ocean_rows(up, fixed, start, forcing, half, -H, 2 * H + 3)
        surface = (surf, -band, whole)
        ocean_rows(up, fixed, half, forcing, surface, -H + 1, 2 * H + 1)
    else:
        surface = start
    step0, step1, step2 = (win, -H, size), (lev1, 1 - H, 7), (lev2, 2 - H, 5)
    step3 = (done, 0, H)
    atmos_rows(up, reals, coef, step0, step1, surface, 1 - H, 7, None, None)
    atmos_rows(up, reals, coef, step1, step2, surface, 2 - H, 5, None, None)
    atmos_rows(up, reals, coef, step2, step3, surface, 0, 3, None, None)
    stores = pool.copies()
    stores.start(lev1.at[:, :, pl.ds(chunk(up, 3, 2, 1 - H, 7), 2)], carry1)
    stores.start(lev2.at[:, :, pl.ds(chunk(up, 2, 2, 2 - H, 5), 2)], carry2)
    if coupled:
        stores.start(surf, surface_out)
    flux_rows(up, reals, step3, surface, (flux, 0, H), 0, H, ensemble)
    stores.wait()


def tile(up, reals, coef, win, lev1, lev2, target, base, surface, edge, valid):
    atmos_rows(up, reals, coef, (win, base - 1, 5), (lev1, base - 2, 5), surface, base, 3, edge, valid)
    atmos_rows(up, reals, coef, (lev1, base - 2, 5), (lev2, base - 3, 5), surface, base - 1, 3, edge, valid)
    atmos_rows(up, reals, coef, (lev2, base - 3, 5), target, surface, base - 2, 3, edge, valid)


def outer_kernel(cfg, ints, reals, coef, a_out, a_high, carry1, carry2, flux_in, sea_low, sea_own, sea_high,
                 done, next1, next2, flux, win, lev1, lev2, sea, sems):
    band, H, ensemble = cfg
    up, valid = ints[0], reals[reals.shape[0] - 1]
    pool = Sems(sems)
    loads = pool.copies()
    loads.start(a_out.at[:, :, pl.ds(chunk(up, 4, 2, 3, 3), 2)], win.at[:, :, pl.ds(chunk(up, 4, 2, 4, 5), 2)])
    loads.start(a_high, win.at[:, :, pl.ds(chunk(up, 6, 3, 4, 5), 3)])
    loads.start(carry1, lev1.at[:, :, pl.ds(chunk(up, 3, 2, 3, 5), 2)])
    loads.start(carry2, lev2.at[:, :, pl.ds(chunk(up, 2, 2, 2, 5), 2)])
    load_three(up, loads, sea, band, sea_low, sea_own, sea_high)
    loads.start(flux_in, flux.at[pl.ds(chunk(up, 0, H, 0, band), H)])
    loads.wait()
    surface = (sea.at[:, 0], -band, 3 * band)
    tile(up, reals, coef, win, lev1, lev2, (done, 3, 3), 5, surface, band, valid)
    stores = pool.copies()
    stores.start(lev1.at[:, :, pl.ds(chunk(up, 6, 2, 3, 5), 2)], next1)
    stores.start(lev2.at[:, :, pl.ds(chunk(up, 5, 2, 2, 5), 2)], next2)
    flux_rows(up, reals, (done, 3, 3), surface, (flux, 0, band), 3, 3, ensemble)
    stores.wait()


def last_kernel(cfg, ints, reals, coef, a_high, a_far, carry1, carry2, sea_low, sea_own, sea_high,
                f_low, f_own, f_high, b_out, b_in, b_carry1, b_carry2, flux_in,
                result, flux, surface_out, win, lev1, lev2, win_b, lev1_b, lev2_b, done, sea, force, middle, surf, sems):
    band, H, ensemble = cfg
    up, valid = ints[0], reals[reals.shape[0] - 1]
    pool = Sems(sems)
    loads = pool.copies()
    whole = 3 * band
    loads.start(a_high.at[:, :, pl.ds(chunk(up, 7, 2, 6, 3), 2)], win.at[:, :, pl.ds(chunk(up, 7, 2, 7, 5), 2)])
    loads.start(a_far, win.at[:, :, pl.ds(chunk(up, 9, 3, 7, 5), 3)])
    loads.start(carry1, lev1.at[:, :, pl.ds(chunk(up, 6, 2, 6, 5), 2)])
    loads.start(carry2, lev2.at[:, :, pl.ds(chunk(up, 5, 2, 5, 5), 2)])
    load_three(up, loads, sea, band, sea_low, sea_own, sea_high)
    load_three(up, loads, force, band, f_low, f_own, f_high)
    loads.start(b_out.at[:, :, pl.ds(chunk(up, 4, 2, 3, 3), 2)], win_b.at[:, :, pl.ds(chunk(up, 4, 2, 4, 5), 2)])
    loads.start(b_carry1, lev1_b.at[:, :, pl.ds(chunk(up, 3, 2, 3, 5), 2)])
    loads.start(b_carry2, lev2_b.at[:, :, pl.ds(chunk(up, 2, 2, 2, 5), 2)])
    loads.start(flux_in, flux.at[pl.ds(chunk(up, 0, H, 0, band), H)])
    loads.wait()
    stores = pool.copies()
    stores.start(b_in, result.at[:, :, pl.ds(chunk(up, 0, H, 0, band), H)])
    start, fixed = (sea.at[:, 0], -band, whole), (sea.at[:, 1], -band, whole)
    forcing, half = (force, -band, whole), (middle, -band, whole)
    surface = (surf, -band, whole)
    ocean_rows(up, fixed, start, forcing, half, -3, 12)
    ocean_rows(up, fixed, half, forcing, surface, -2, 10)
    tile(up, reals, coef, win, lev1, lev2, (win_b, 4, 5), 8, start, band, valid)
    tile(up, reals, coef, win_b, lev1_b, lev2_b, (done, 3, 3), 5, surface, band, valid)
    stores.start(done, result.at[:, :, pl.ds(chunk(up, 3, H, 0, band), H)])
    stores.start(surf, surface_out)
    flux_rows(up, reals, (done, 3, 3), surface, (flux, 0, band), 3, 3, ensemble)
    stores.wait()


def ocean_kernel(cfg, ints, surface_in, sea_low, sea_own, sea_high, f_low, f_own, f_high, out,
                 sea, surf, force, middle, final, sems):
    band, H, tile_width = cfg
    up = ints[0]
    pool = Sems(sems)
    loads = pool.copies()
    whole = 3 * band
    load_three(up, loads, sea, band, sea_low, sea_own, sea_high)
    loads.start(surface_in, surf)
    loads.start(f_low, force.at[pl.ds(chunk(up, -1, 1, -1, band + 2), 1)])
    loads.start(f_own, force.at[pl.ds(1, band)])
    loads.start(f_high, force.at[pl.ds(chunk(up, band, 1, -1, band + 2), 1)])
    loads.wait()
    fixed, ocean = (sea.at[:, 1], -band, whole), (surf, -band, whole)
    forcing, half = (force, -1, band + 2), (middle, -1, band + 2)
    ocean_rows(up, fixed, ocean, forcing, half, -1, band + 2)
    ocean_rows(up, fixed, half, forcing, (final, 0, band), 0, band)
    if tile_width is None:
        out[...] = final[...]
    else:
        lon = final.shape[2]
        for row in range(band):
            for c in range(2):
                for part in range(tile_width // lon):
                    line = c * QUARTERS + ints[1] * (tile_width // lon) + part
                    out[row, c : c + 1, part * lon : (part + 1) * lon] = final[row, pl.ds(line, 1), :]


def call(kernel, name, outs, scratch, args, copies, flops=0):
    kinds = {"any": ANY, "vmem": VMEM, "smem": SMEM}
    return pl.pallas_call(
        kernel,
        name=name,
        out_shape=[jax.ShapeDtypeStruct(shape, jnp.float32) for _, shape in outs],
        in_specs=[kinds[kind] for kind, _ in args],
        out_specs=[kinds[kind] for kind, _ in outs],
        scratch_shapes=[pltpu.VMEM(shape, jnp.float32) for shape in scratch] + [pltpu.SemaphoreType.DMA((copies,))],
        compiler_params=pltpu.CompilerParams(vmem_limit_bytes=24 * 1024 * 1024),
        cost_estimate=pl.CostEstimate(flops=flops, bytes_accessed=4 * 1024 * 1024, transcendentals=0),
    )(*[value for _, value in args])


def lookup(parameter_index, parameter_table):
    onehot = (
        parameter_index[:, None] == jnp.arange(parameter_table.shape[0], dtype=jnp.int32)[None, :]
    ).astype(jnp.float32)
    picked = jnp.dot(
        onehot, parameter_table, precision=lax.Precision.HIGHEST, preferred_element_type=jnp.float32
    )
    return (0.6 * picked[:, 0], 2.0 * jnp.transpose(picked[:, 1:3]))


def mixing(level_mix, exchange):
    levels = level_mix.shape[0]
    ids = jnp.arange(levels)
    pick = (ids[None, None, :] == (ids[None, :, None] + ids[:, None, None]) % levels).astype(jnp.float32)
    whole = level_mix + jnp.eye(levels, dtype=jnp.float32)
    turned = jnp.sum(pick * whole[None], axis=2)
    scale = jnp.where(ids == 0, 1.0 - exchange[:, :, None], 1.0)
    coef = turned[None, None] * scale[:, :, None, :]
    return jnp.broadcast_to(coef[..., None], coef.shape + (LANES,))


def body(atmosphere, ocean_state, viscosity, sea_mask, parameter_index, parameter_table, level_mix):
    H = ASTEPS
    fields, members, levels, band, lon = atmosphere.shape
    width = ocean_state.shape[2]
    sides, bands = lax.axis_size("member"), lax.axis_size("lat")
    ensemble = members * sides
    position = lax.axis_index("lat")
    side = lax.axis_index("member")
    up = position % 2
    near = [(i, i + 1) for i in range(0, bands, 2)]
    near += [(b, a) for a, b in near]
    far = [(i, i + 1) for i in range(1, bands - 1, 2)]
    far += [(b, a) for a, b in far]
    other = [(0, 1), (1, 0)]

    def to_near(x):
        return lax.ppermute(x, "lat", near)

    def to_far(x):
        return lax.ppermute(x, "lat", far)

    def total(x):
        if sides == 2:
            return x + lax.ppermute(x, "member", other)
        return lax.psum(x, "member")

    def full_rows(x):
        if sides == 2:
            y = lax.ppermute(x, "member", other)
            low, high = jnp.where(side == 0, x, y), jnp.where(side == 0, y, x)
            return jnp.concatenate([low, high], axis=2)
        return lax.all_gather(x, "member", axis=2, tiled=True)

    state = jnp.transpose(atmosphere, (0, 1, 3, 2, 4))
    a_out = lax.dynamic_slice_in_dim(state, up * H, H, 2)
    a_in = lax.dynamic_slice_in_dim(state, (1 - up) * H, H, 2)
    a_low = to_near(a_in)

    ocean_state, viscosity, a_out = lax.optimization_barrier((ocean_state, viscosity, a_out))
    tile_fields = jnp.concatenate([jnp.transpose(ocean_state, (1, 0, 2)), viscosity[:, None]], axis=1)
    a_high = to_far(a_out)
    packed = (band, 1, fields * QUARTERS, lon // QUARTERS)
    sea_tile = full_rows(tile_fields)
    masked = jnp.concatenate([sea_tile[:, 2:], sea_mask.astype(jnp.float32)[:, None]], axis=1)
    sea_own = jnp.concatenate([sea_tile[:, :2].reshape(packed), masked.reshape(packed)], axis=1)
    sea_low, sea_high = to_near(sea_own), to_far(sea_own)

    sea_high, far_rows = lax.optimization_barrier((sea_high, a_in))
    a_far = to_far(far_rows)
    diffusivity, exchange = lookup(parameter_index, parameter_table)
    coef = mixing(level_mix, exchange)
    valid = jnp.where(up == 1, position < bands - 1, position > 0).astype(jnp.float32)
    reals = jnp.concatenate([diffusivity, exchange.reshape(-1), valid[None]])
    ints = jnp.stack([up, side]).astype(jnp.int32)
    common = [("smem", ints), ("smem", reals), ("vmem", coef)]
    seas = [("any", sea_low), ("any", sea_own), ("any", sea_high)]

    def band_shape(n):
        return (n, fields * QUARTERS, lon // QUARTERS)

    sea_shape = (3 * band, 2, fields * QUARTERS, lon // QUARTERS)

    def rows(n):
        return (fields, members, n, levels, lon)

    cfg = (band, H, ensemble)
    unit = members * fields * levels * lon * 30

    def inner(coupled, low, inside, outside, sea3, force3, name):
        outs = [("vmem", rows(H)), ("any", rows(2)), ("any", rows(2)), ("vmem", band_shape(H))]
        scratch = [rows(3 * H), rows(7), rows(5), sea_shape]
        if coupled:
            scratch += [band_shape(3 * band)] * 3
            outs += [("any", band_shape(3 * band))]
        args = common + [("any", low), ("any", inside), ("any", outside)] + sea3 + force3
        return call(functools.partial(inner_kernel, cfg, coupled), name, outs, scratch, args, 16, 15 * unit)

    b_in, carry1, carry2, flux = inner(False, a_low, a_in, a_out, seas[:2] + [("any", sea_own)], [], "inner_first")
    b_low = to_near(b_in)
    b_out, carry1, carry2, flux = call(
        functools.partial(outer_kernel, cfg), "outer_first",
        [("vmem", rows(H)), ("any", rows(2)), ("any", rows(2)), ("vmem", band_shape(band))],
        [rows(5), rows(5), rows(5), sea_shape],
        common + [("any", a_out), ("any", a_high), ("any", carry1), ("any", carry2), ("any", flux)] + seas, 16, 9 * unit)
    f_own = total(flux)
    f_low, f_high = to_near(f_own), to_far(f_own)
    c_in, b_carry1, b_carry2, flux, _ = inner(
        True, b_low, b_in, b_out, seas,
        [("any", f_low), ("any", f_own), ("any", f_own)], "inner_second")
    result, flux, surface = call(
        functools.partial(last_kernel, cfg), "outer_second",
        [("any", rows(band)), ("vmem", band_shape(band)), ("any", band_shape(3 * band))],
        [rows(5)] * 6 + [rows(H), sea_shape] + [band_shape(3 * band)] * 3,
        common + [("any", a_high), ("any", a_far), ("any", carry1), ("any", carry2)] + seas
        + [("any", f_low), ("any", f_own), ("any", f_high), ("any", b_out), ("any", c_in), ("any", b_carry1), ("any", b_carry2), ("any", flux)],
        24, 18 * unit)
    g_own = total(flux)
    g_low = to_near(lax.dynamic_slice_in_dim(g_own, (1 - up) * (band - 1), 1, 0))
    g_high = to_far(lax.dynamic_slice_in_dim(g_own, up * (band - 1), 1, 0))
    inside_kernel = width % (lon // QUARTERS) == 0
    (ocean,) = call(
        functools.partial(ocean_kernel, (band, H, width if inside_kernel else None)), "ocean_last",
        [("vmem", (band, fields, width) if inside_kernel else band_shape(band))],
        [sea_shape, band_shape(3 * band), band_shape(band + 2), band_shape(band + 2), band_shape(band)],
        [("smem", ints), ("any", surface)] + seas + [("any", g_low), ("any", g_own), ("any", g_high)], 8)
    if not inside_kernel:
        ocean = lax.dynamic_slice_in_dim(ocean.reshape(band, fields, lon), side * width, width, 2)
    return (jnp.transpose(result, (0, 1, 3, 2, 4)), jnp.transpose(ocean, (1, 0, 2)))


def solution(mesh):
    return jax.shard_map(
        body,
        mesh=mesh,
        in_specs=(
            P(None, "member", None, "lat", None),
            P(None, "lat", "member"),
            P("lat", "member"),
            P("lat", None),
            P("member"),
            P(),
            P(),
        ),
        out_specs=(P(None, "member", None, "lat", None), P(None, "lat", "member")),
        check_vma=False,
    )
```

```python
import functools

import jax
import jax.numpy as jnp
from jax import lax
from jax.experimental import pallas as pl
from jax.experimental.pallas import tpu as pltpu
from jax.sharding import PartitionSpec as P

ASTEPS = 3
OSTEPS = 2
COUPLE = 2

ADVECTION = 0.1
OCEAN_GAIN = 0.5
OCEAN_DIFFUSION = 0.15

ANY = pl.BlockSpec(memory_space=pl.ANY)
VMEM = pl.BlockSpec(memory_space=pltpu.VMEM)
SMEM = pl.BlockSpec(memory_space=pltpu.SMEM)
LANES = 128
QUARTERS = 4


def place(up, row, base, count):
    return jnp.where(up == 1, row - base, count - 1 - (row - base))


class Rows:
    def __init__(self, up, *pieces):
        self.up, self.pieces = up, pieces

    def at(self, row):
        for ref, base, count in self.pieces:
            if base <= row < base + count:
                return ref, place(self.up, row, base, count)
        raise IndexError(row)


def sea_piece(ref, row, c, t, lon):
    per = lon // QUARTERS // LANES
    line, part = c * QUARTERS + t // per, t % per
    return ref[row, line : line + 1, part * LANES : (part + 1) * LANES]


def atmos_rows(reals, coef, source, target, surface, rows, edge=None, valid=None):
    level = lax.broadcasted_iota(jnp.int32, (8, LANES), 0)
    lane = lax.broadcasted_iota(jnp.int32, (8, LANES), 1)
    for row in rows:
        src, here = source.at(row)
        src_s, south = source.at(row - 1)
        src_n, north = source.at(row + 1)
        dst, there = target.at(row)
        srf, sea = surface.at(row)
        members, lon = src.shape[1], src.shape[4]
        tiles = lon // LANES
        for m in range(members):
            diffusivity = reals[m]
            keep = 1.0 - 4.0 * diffusivity
            centres, easts, wests = {}, {}, {}
            for step in range(tiles + 2):
                ahead = step % tiles
                for c in (1, 0):
                    if (c, ahead) not in centres:
                        piece = src[c, m, here, :, ahead * LANES : (ahead + 1) * LANES]
                        centres[c, ahead] = piece
                        easts[c, ahead] = pltpu.roll(piece, LANES - 1, 1)
                        wests[c, ahead] = pltpu.roll(piece, 1, 1)
                if step < 2:
                    continue
                t = (step - 1) % tiles
                before, after = (t - 1) % tiles, (t + 1) % tiles
                span = slice(t * LANES, (t + 1) * LANES)
                wind = (0.5 * ADVECTION) * centres[1, t]
                for c in (1, 0):
                    eastern = jnp.where(lane == LANES - 1, easts[c, after], easts[c, t])
                    western = jnp.where(lane == 0, wests[c, before], wests[c, t])
                    beside = src_s[c, m, south, :, span] + src_n[c, m, north, :, span]
                    part = (
                        keep * centres[c, t]
                        + diffusivity * (beside + (eastern + western))
                        - wind * (eastern - western)
                    )
                    total = coef[c, m, 0] * part
                    for d in range(1, 8):
                        total += coef[c, m, d] * pltpu.roll(part, 8 - d, 0)
                    relax = jnp.where(level == 0, reals[members + c * members + m], 0.0)
                    total += relax * sea_piece(srf, sea, c, t, lon)
                    if edge is not None and row >= edge:
                        total = total * valid
                    dst[c, m, there, :, span] = total


def flux_rows(reals, state, surface, out, rows, ensemble):
    for row in rows:
        st, at = state.at(row)
        srf, sea = surface.at(row)
        ref, to = out.at(row)
        members, lon = st.shape[1], st.shape[4]
        per = lon // QUARTERS // LANES
        for c in range(2):
            for t in range(lon // LANES):
                s = sea_piece(srf, sea, c, t, lon)
                flux = jnp.zeros_like(s)
                for m in range(members):
                    flux += reals[members + c * members + m] * (st[c, m, at, 0:1, t * LANES : (t + 1) * LANES] - s)
                line, part = c * QUARTERS + t // per, t % per
                ref[to, line : line + 1, part * LANES : (part + 1) * LANES] = flux * (1.0 / ensemble)


def ocean_rows(sea, ocean, forcing, target, rows):
    for row in rows:
        src, here = ocean.at(row)
        src_s, south = ocean.at(row - 1)
        src_n, north = ocean.at(row + 1)
        fixed, cell = sea.at(row)
        frc, force = forcing.at(row)
        dst, to = target.at(row)
        centre = src[here]
        lines, lon = centre.shape
        line = lax.broadcasted_iota(jnp.int32, (lines, lon), 0)
        lane = lax.broadcasted_iota(jnp.int32, (lines, lon), 1)
        quarter = line % QUARTERS
        both = fixed[cell]
        turned = pltpu.roll(both, QUARTERS, 0)
        mask = jnp.where(line < QUARTERS, turned, both)
        rate = jnp.where(line < QUARTERS, OCEAN_DIFFUSION, turned)
        eastern, western = pltpu.roll(centre, lon - 1, 1), pltpu.roll(centre, 1, 1)
        after = jnp.where(quarter == QUARTERS - 1, pltpu.roll(eastern, QUARTERS - 1, 0), pltpu.roll(eastern, lines - 1, 0))
        before = jnp.where(quarter == 0, pltpu.roll(western, lines - QUARTERS + 1, 0), pltpu.roll(western, 1, 0))
        eastern = jnp.where(lane == lon - 1, after, eastern)
        western = jnp.where(lane == 0, before, western)
        laplace = (eastern + western) + (src_s[south] + src_n[north]) - 4.0 * centre
        dst[to] = centre + mask * (OCEAN_GAIN * frc[force] + rate * laplace)


def started(source, target, sem):
    copy = pltpu.make_async_copy(source, target, sem)
    copy.start()
    return copy


def sea_of(up, band, low, own, high, part):
    return Rows(up, (low.at[:, part], -band, band), (own.at[:, part], 0, band), (high.at[:, part], band, band))


def gather_columns(width, ints, ocean, viscosity, mask, out):
    for row in range(ocean.shape[0]):
        out[row, 0:2, :] = ocean[row]
        out[row, 2:3, :] = viscosity[row : row + 1, :]
        piece = mask[row : row + 1, pl.ds(pl.multiple_of(ints[1] * width, LANES), width)]
        out[row, 3:4, :] = piece.astype(jnp.float32)


def pack_rows(cfg, ints, own, other, out):
    side = ints[1]
    rows, _, lines, size = out.shape
    parts = own.shape[2] // size
    for row in range(rows):
        for field in range(4):
            for part in range(parts):
                line = (field % 2) * QUARTERS + part
                for ref, half in ((own, side), (other, 1 - side)):
                    out[row, field // 2, pl.ds(line + half * parts, 1), :] = ref[
                        row, field : field + 1, part * size : (part + 1) * size
                    ]


def inner_first(cfg, ints, reals, coef, a_low, a_in, a_out, sea_low, sea_own,
                done, carry1, carry2, flux, lev1, lev2, keep1, keep2, sems):
    band, H, ensemble = cfg
    up = ints[0]
    surface = Rows(up, (sea_low.at[:, 0], -band, band), (sea_own.at[:, 0], 0, band))
    inner(up, cfg, reals, coef, surface, a_low, a_in, a_out, done, carry1, carry2, flux, lev1, lev2, keep1, keep2, sems)


def inner(up, cfg, reals, coef, surface, a_low, a_in, a_out, done, carry1, carry2, flux, lev1, lev2, keep1, keep2, sems):
    band, H, ensemble = cfg
    step0 = Rows(up, (a_low, -H, H), (a_in, 0, H), (a_out, H, H))
    step1 = Rows(up, (lev1, -2, 5), (keep1, 3, 2))
    step2 = Rows(up, (lev2, -1, 3), (keep2, 2, 2))
    step3 = Rows(up, (done, 0, H))
    atmos_rows(reals, coef, step0, step1, surface, range(-2, 5))
    first = started(keep1, carry1, sems.at[0])
    atmos_rows(reals, coef, step1, step2, surface, range(-1, 4))
    second = started(keep2, carry2, sems.at[1])
    atmos_rows(reals, coef, step2, step3, surface, range(0, 3))
    flux_rows(reals, step3, surface, Rows(up, (flux, 0, H)), range(H), ensemble)
    first.wait()
    second.wait()


def inner_second(cfg, ints, reals, coef, a_low, a_in, a_out, sea_low, sea_own, sea_high, f_low, f_own,
                 done, carry1, carry2, flux, surf_out, surf, middle, lev1, lev2, keep1, keep2, sems):
    band, H, ensemble = cfg
    up = ints[0]
    start, fixed = (sea_of(up, band, sea_low, sea_own, sea_high, part) for part in range(2))
    forcing = Rows(up, (f_low, -band, band), (f_own, 0, band))
    half, surface = Rows(up, (middle, -3, 9)), Rows(up, (surf, -2, 7))
    ocean_rows(fixed, start, forcing, half, range(-3, 6))
    ocean_rows(fixed, half, forcing, surface, range(-2, 5))
    third = started(surf, surf_out, sems.at[2])
    inner(up, cfg, reals, coef, surface, a_low, a_in, a_out, done, carry1, carry2, flux, lev1, lev2, keep1, keep2, sems)
    third.wait()


def outer_first(cfg, ints, reals, coef, a_out, a_high, carry1, carry2, flux_in, sea_own, sea_high,
                done, next1, next2, flux, lev1, lev2, keep1, keep2, made1, made2, part, sems):
    band, H, ensemble = cfg
    up, valid = ints[0], reals[reals.shape[0] - 1]
    surface = Rows(up, (sea_own.at[:, 0], 0, band), (sea_high.at[:, 0], band, band))
    step0 = Rows(up, (a_out, 3, 3), (a_high, 6, 3))
    loads = [started(carry1, keep1, sems.at[0]), started(carry2, keep2, sems.at[1]), started(flux_in, part, sems.at[2])]
    step1 = Rows(up, (keep1, 3, 2), (lev1, 5, 1), (made1, 6, 2))
    step2 = Rows(up, (keep2, 2, 2), (lev2, 4, 1), (made2, 5, 2))
    step3 = Rows(up, (done, 3, 3))
    atmos_rows(reals, coef, step0, step1, surface, range(5, 8), band, valid)
    first = started(made1, next1, sems.at[3])
    for copy in loads:
        copy.wait()
    atmos_rows(reals, coef, step1, step2, surface, range(4, 7), band, valid)
    second = started(made2, next2, sems.at[4])
    atmos_rows(reals, coef, step2, step3, surface, range(3, 6), band, valid)
    join_flux(up, H, band, part, flux)
    flux_rows(reals, step3, surface, Rows(up, (flux, 0, band)), range(3, 6), ensemble)
    first.wait()
    second.wait()


def join_flux(up, H, band, flux_in, flux):
    source, target = Rows(up, (flux_in, 0, H)), Rows(up, (flux, 0, band))
    for row in range(H):
        (src, here), (dst, there) = source.at(row), target.at(row)
        dst[there] = src[here]


def outer_halo(cfg, ints, reals, coef, a_high, a_far, carry1, carry2, sea_high, done, lev1, lev2, keep1, keep2, sems):
    band, H, ensemble = cfg
    up, valid = ints[0], reals[reals.shape[0] - 1]
    surface = Rows(up, (sea_high.at[:, 0], band, band))
    step0 = Rows(up, (a_high, 6, 3), (a_far, 9, 3))
    loads = [started(carry1, keep1, sems.at[0]), started(carry2, keep2, sems.at[1])]
    step1 = Rows(up, (keep1, 6, 2), (lev1, 8, 3))
    step2 = Rows(up, (keep2, 5, 2), (lev2, 7, 3))
    step3 = Rows(up, (done, 6, 3))
    atmos_rows(reals, coef, step0, step1, surface, range(8, 11), band, valid)
    for copy in loads:
        copy.wait()
    atmos_rows(reals, coef, step1, step2, surface, range(7, 10), band, valid)
    atmos_rows(reals, coef, step2, step3, surface, range(6, 9), band, valid)


def outer_second(cfg, ints, reals, coef, b_out, b_high, b_carry1, b_carry2, b_in, flux_in, s_in,
                 sea_low, sea_own, sea_high, f_low, f_own, f_high,
                 result, flux, s_out, middle, lev1, lev2, done, keep1, keep2, part, s_kept, sems):
    band, H, ensemble = cfg
    up, valid = ints[0], reals[reals.shape[0] - 1]
    s_load = started(s_in, s_kept, sems.at[2])
    loads = [started(b_carry1, keep1, sems.at[3]), started(b_carry2, keep2, sems.at[4]), started(flux_in, part, sems.at[5])]
    first = pltpu.make_async_copy(b_in, result.at[:, :, pl.ds(jnp.where(up == 1, 0, H), H)], sems.at[0])
    first.start()
    start, fixed = (sea_of(up, band, sea_low, sea_own, sea_high, part) for part in range(2))
    forcing = Rows(up, (f_own, 0, band), (f_high, band, band))
    half = Rows(up, (middle, 4, 5))
    surface = Rows(up, (s_kept, -2, 7), (s_out, 5, 3))
    ocean_rows(fixed, start, forcing, half, range(4, 9))
    ocean_rows(fixed, half, forcing, surface, range(5, 8))
    step0 = Rows(up, (b_out, 3, 3), (b_high, 6, 3))
    step1 = Rows(up, (keep1, 3, 2), (lev1, 5, 3))
    step2 = Rows(up, (keep2, 2, 2), (lev2, 4, 3))
    step3 = Rows(up, (done, 3, 3))
    atmos_rows(reals, coef, step0, step1, surface, range(5, 8), band, valid)
    s_load.wait()
    for copy in loads:
        copy.wait()
    atmos_rows(reals, coef, step1, step2, surface, range(4, 7), band, valid)
    atmos_rows(reals, coef, step2, step3, surface, range(3, 6), band, valid)
    second = pltpu.make_async_copy(done, result.at[:, :, pl.ds(jnp.where(up == 1, H, 0), H)], sems.at[1])
    second.start()
    join_flux(up, H, band, part, flux)
    flux_rows(reals, step3, surface, Rows(up, (flux, 0, band)), range(3, 6), ensemble)
    first.wait()
    second.wait()


def ocean_last(cfg, ints, s_in, s_out, sea_low, sea_own, sea_high, f_low, f_own, f_high, out, middle, final, s_kept, sems):
    band, H, width = cfg
    up = ints[0]
    fixed = sea_of(up, band, sea_low, sea_own, sea_high, 1)
    started(s_in, s_kept, sems.at[0]).wait()
    surface = Rows(up, (s_kept, -2, 7), (s_out, 5, 3))
    forcing = Rows(up, (f_low, -1, 1), (f_own, 0, band), (f_high, band, 1))
    half = Rows(up, (middle, -1, band + 2))
    ocean_rows(fixed, surface, forcing, half, range(-1, band + 1))
    if width is None:
        ocean_rows(fixed, half, forcing, Rows(up, (out, 0, band)), range(band))
        return
    ocean_rows(fixed, half, forcing, Rows(up, (final, 0, band)), range(band))
    lon = final.shape[2]
    for row in range(band):
        for c in range(2):
            for part in range(width // lon):
                line = c * QUARTERS + ints[1] * (width // lon) + part
                out[row, c : c + 1, part * lon : (part + 1) * lon] = final[row, pl.ds(line, 1), :]


def call(kernel, cfg, outs, scratch, args, copies=0, flops=0):
    kinds = {"any": ANY, "vmem": VMEM, "smem": SMEM}
    return pl.pallas_call(
        functools.partial(kernel, cfg),
        name=kernel.__name__,
        out_shape=[jax.ShapeDtypeStruct(shape, jnp.float32) for _, shape in outs],
        in_specs=[kinds[kind] for kind, _ in args],
        out_specs=[kinds[kind] for kind, _ in outs],
        scratch_shapes=[pltpu.VMEM(shape, jnp.float32) for shape in scratch]
        + [pltpu.SemaphoreType.DMA((copies,))] * (copies > 0),
        compiler_params=pltpu.CompilerParams(vmem_limit_bytes=20 * 1024 * 1024),
        cost_estimate=pl.CostEstimate(flops=flops, bytes_accessed=4 * 1024 * 1024, transcendentals=0),
    )(*[value for _, value in args])


def lookup(parameter_index, parameter_table):
    onehot = (
        parameter_index[:, None] == jnp.arange(parameter_table.shape[0], dtype=jnp.int32)[None, :]
    ).astype(jnp.float32)
    picked = jnp.dot(
        onehot, parameter_table, precision=lax.Precision.HIGHEST, preferred_element_type=jnp.float32
    )
    return (0.6 * picked[:, 0], 2.0 * jnp.transpose(picked[:, 1:3]))


def mixing(level_mix, exchange):
    levels = level_mix.shape[0]
    ids = jnp.arange(levels)
    pick = (ids[None, None, :] == (ids[None, :, None] + ids[:, None, None]) % levels).astype(jnp.float32)
    whole = level_mix + jnp.eye(levels, dtype=jnp.float32)
    turned = jnp.sum(pick * whole[None], axis=2)
    scale = jnp.where(ids == 0, 1.0 - exchange[:, :, None], 1.0)
    coef = turned[None, None] * scale[:, :, None, :]
    return jnp.broadcast_to(coef[..., None], coef.shape + (LANES,))


def body(atmosphere, ocean_state, viscosity, sea_mask, parameter_index, parameter_table, level_mix):
    H = ASTEPS
    fields, members, levels, band, lon = atmosphere.shape
    width = ocean_state.shape[2]
    sides, bands = lax.axis_size("member"), lax.axis_size("lat")
    ensemble = members * sides
    position = lax.axis_index("lat")
    side = lax.axis_index("member")
    up = position % 2
    near = [(i, i + 1) for i in range(0, bands, 2)]
    near += [(b, a) for a, b in near]
    far = [(i, i + 1) for i in range(1, bands - 1, 2)]
    far += [(b, a) for a, b in far]
    other = [(0, 1), (1, 0)]

    def rows(n):
        return (fields, members, n, levels, lon)

    def band_shape(n):
        return (n, fields * QUARTERS, lon // QUARTERS)

    def vmem(*values):
        return [("vmem", value) for value in values]

    def anywhere(*values):
        return [("any", value) for value in values]

    def to_near(x):
        return lax.ppermute(x, "lat", near)

    def to_far(x):
        return lax.ppermute(x, "lat", far)

    def total(x):
        if sides == 2:
            return x + lax.ppermute(x, "member", other)
        return lax.psum(x, "member")

    def total_beside(x, work):
        if sides == 2:
            y, work = lax.optimization_barrier((lax.ppermute(x, "member", other), work))
            return x + y, work
        return lax.psum(x, "member"), work

    def full_rows(x):
        if sides == 2:
            y = lax.ppermute(x, "member", other)
            if whole_quarters:
                (packed,) = call(pack_rows, None, vmem((band, 2, fields * QUARTERS, lon // QUARTERS)), [], [("smem", ints)] + vmem(x, y))
                return packed
            low, high = jnp.where(side == 0, x, y), jnp.where(side == 0, y, x)
            whole = jnp.concatenate([low, high], axis=2)
        else:
            whole = lax.all_gather(x, "member", axis=2, tiled=True)
        return whole.reshape(band, 2, fields * QUARTERS, lon // QUARTERS)

    state = jnp.transpose(atmosphere, (0, 1, 3, 2, 4))
    ints = jnp.stack([up, side]).astype(jnp.int32)
    whole_quarters = width % (lon // QUARTERS) == 0
    turned_ocean = jnp.transpose(ocean_state, (1, 0, 2))
    if width % LANES == 0:
        (columns,) = call(
            gather_columns, width, vmem((band, 4, width)), [],
            [("smem", ints)] + vmem(turned_ocean, viscosity, sea_mask))
    else:
        mask = lax.dynamic_slice_in_dim(sea_mask, side * width, width, 1).astype(jnp.float32)
        columns = jnp.concatenate([turned_ocean, viscosity[:, None], mask[:, None]], axis=1)
    far_columns = to_far(columns)
    columns, start = lax.optimization_barrier((columns, up))
    a_out = lax.dynamic_slice_in_dim(state, start * H, H, 2)
    a_high = to_far(a_out)
    later, a_out = lax.optimization_barrier((start, a_out))
    a_in = lax.dynamic_slice_in_dim(state, (1 - later) * H, H, 2)
    a_low = to_near(a_in)
    sea_own = full_rows(columns)
    sea_low = to_near(sea_own)
    far_columns, a_low = lax.optimization_barrier((far_columns, a_low))
    sea_high = full_rows(far_columns)

    diffusivity, exchange = lookup(parameter_index, parameter_table)
    coef = mixing(level_mix, exchange)
    valid = jnp.where(up == 1, position < bands - 1, position > 0).astype(jnp.float32)
    reals = jnp.concatenate([diffusivity, exchange.reshape(-1), valid[None]])
    common = [("smem", ints), ("smem", reals), ("vmem", coef)]
    cfg = (band, H, ensemble)
    unit = members * fields * levels * lon * 30
    carries = anywhere(rows(2), rows(2))
    inner_outs = vmem(rows(H)) + carries + vmem(band_shape(H))
    kept = [rows(2), rows(2)]

    b_in, carry1, carry2, flux = call(
        inner_first, cfg, inner_outs, [rows(5), rows(3)] + kept,
        common + vmem(a_low, a_in, a_out, sea_low, sea_own), 2, flops=15 * unit)
    a_far = to_far(a_in)
    b_low = to_near(b_in)
    b_out, carry1, carry2, flux = call(
        outer_first, cfg, vmem(rows(H)) + carries + vmem(band_shape(band)), [rows(1), rows(1)] + kept * 2 + [band_shape(H)],
        common + vmem(a_out, a_high) + anywhere(carry1, carry2, flux) + vmem(sea_own, sea_high), 5, flops=9 * unit)
    (b_high,) = call(
        outer_halo, cfg, vmem(rows(H)), [rows(3), rows(3)] + kept,
        common + vmem(a_high, a_far) + anywhere(carry1, carry2) + vmem(sea_high), 2, flops=9 * unit)
    f_own, b_high = total_beside(flux, b_high)
    f_low, f_high = to_near(f_own), to_far(f_own)
    c_in, b_carry1, b_carry2, flux, s_in = call(
        inner_second, cfg, inner_outs + anywhere(band_shape(7)), [band_shape(7), band_shape(9), rows(5), rows(3)] + kept,
        common + vmem(b_low, b_in, b_out, sea_low, sea_own, sea_high, f_low, f_own), 3, flops=15 * unit)
    result, flux, s_out = call(
        outer_second, cfg, [("any", rows(band))] + vmem(band_shape(band), band_shape(3)),
        [band_shape(5), rows(3), rows(3), rows(3)] + kept + [band_shape(H), band_shape(7)],
        common + vmem(b_out, b_high) + anywhere(b_carry1, b_carry2, c_in, flux, s_in)
        + vmem(sea_low, sea_own, sea_high, f_low, f_own, f_high),
        copies=6, flops=9 * unit)
    g_own = total(flux)
    g_low = to_near(lax.dynamic_slice_in_dim(g_own, (1 - up) * (band - 1), 1, 0))
    g_high = to_far(lax.dynamic_slice_in_dim(g_own, up * (band - 1), 1, 0))
    (ocean,) = call(
        ocean_last, (band, H, width if whole_quarters else None),
        vmem((band, fields, width) if whole_quarters else band_shape(band)), [band_shape(band + 2), band_shape(band), band_shape(7)],
        [("smem", ints)] + anywhere(s_in) + vmem(s_out, sea_low, sea_own, sea_high, g_low, g_own, g_high), 1)
    if not whole_quarters:
        ocean = lax.dynamic_slice_in_dim(ocean.reshape(band, fields, lon), side * width, width, 2)
    return (jnp.transpose(result, (0, 1, 3, 2, 4)), jnp.transpose(ocean, (1, 0, 2)))


def solution(mesh):
    return jax.shard_map(
        body,
        mesh=mesh,
        in_specs=(
            P(None, "member", None, "lat", None),
            P(None, "lat", "member"),
            P("lat", "member"),
            P("lat", None),
            P("member"),
            P(),
            P(),
        ),
        out_specs=(P(None, "member", None, "lat", None), P(None, "lat", "member")),
        check_vma=False,
    )
```
